768 devices in a mesh: rep: 48 (over z, x), fsdp: 16 (over y, core).
Axes of the slice: x: 4, y: 8, z: 12, core: 2. Of those that a mesh axis runs over, the one named last changes fastest.
Arguments:
- grad_parts: bfloat16 [48, 48, 512, 512], P('rep', None, 'fsdp'), may hold values from -0.09375 to 0.09375
- owner: int32 [48], P('rep'), may hold values from 0 to 15
- left_stat: bfloat16 [48, 16, 512, 512], P('rep', 'fsdp'), may hold values from -1 to 5, as said below
- right_stat: bfloat16 [48, 16, 512, 512], P('rep', 'fsdp'), may hold values from -1 to 5, as said below
- left_root: bfloat16 [48, 16, 512, 512], P('rep', 'fsdp'), may hold values from -1 to 4, as said below
- right_root: bfloat16 [48, 16, 512, 512], P('rep', 'fsdp'), may hold values from -1 to 4, as said below
Outputs:
- left_new: bfloat16 [48, 16, 512, 512], P('rep', 'fsdp')
- right_new: bfloat16 [48, 16, 512, 512], P('rep', 'fsdp')
- update: bfloat16 [48, 512, 512], P('rep', 'fsdp')
The draws below stay inside these ranges and needn't reach their ends.
Inputs may be any that keep to these rules, and one draw needn't show every extreme that they name: `left_stat`: symmetric. `right_stat`: symmetric. `left_root`: symmetric. `right_root`: symmetric.
All inputs are finite; a program needn't handle non-finite values.
Results may differ from the reference program's by a relative error of at most 0.0057.
Values may be sent and summed in bfloat16 or wider, within the bound.
No kernel may reach another device: no remote copies, remote signals or barrier semaphores. Data moves between devices by JAX's collectives and lax.ppermute only.
A program may use at most 32 MiB of HBM per device.

```python
import math
import jax
import jax.numpy as jnp
from jax import lax

BLK = 512
NB = 48
N_REP = 48
N_FSDP = 16


def symmetric_noise(key, spread):
    raw = jax.random.uniform(key, (N_REP, N_FSDP, BLK, BLK), jnp.float32, -1.0, 1.0)
    return spread * (raw + jnp.swapaxes(raw, 2, 3))


def unit_diagonal():
    rows = lax.broadcasted_iota(jnp.int32, (BLK, BLK), 0)
    cols = lax.broadcasted_iota(jnp.int32, (BLK, BLK), 1)
    return (rows == cols).astype(jnp.float32)


def log_even(key, low, high):
    return jnp.exp(jax.random.uniform(key, (N_REP, N_FSDP, BLK), jnp.float32, math.log(low), math.log(high)))


def draw_left_stat(key, part):
    key = jax.random.fold_in(key, 11)
    noise_key, diag_key = jax.random.split(key)
    spread = 0.05
    diagonal = log_even(diag_key, 0.5, 4.0)
    return (symmetric_noise(noise_key, spread) + diagonal[..., None] * unit_diagonal()).astype(jnp.bfloat16)


def draw_right_stat(key, part):
    key = jax.random.fold_in(key, 12)
    noise_key, diag_key = jax.random.split(key)
    spread = 0.05
    diagonal = log_even(diag_key, 0.5, 4.0)
    return (symmetric_noise(noise_key, spread) + diagonal[..., None] * unit_diagonal()).astype(jnp.bfloat16)


def draw_left_root(key, part):
    key = jax.random.fold_in(key, 13)
    noise_key, diag_key = jax.random.split(key)
    spread = 0.735 / math.sqrt(BLK)
    diagonal = log_even(diag_key, 0.3, 3.0)
    return (symmetric_noise(noise_key, spread) + diagonal[..., None] * unit_diagonal()).astype(jnp.bfloat16)


def draw_right_root(key, part):
    key = jax.random.fold_in(key, 14)
    noise_key, diag_key = jax.random.split(key)
    spread = 0.735 / math.sqrt(BLK)
    diagonal = log_even(diag_key, 0.3, 3.0)
    return (symmetric_noise(noise_key, spread) + diagonal[..., None] * unit_diagonal()).astype(jnp.bfloat16)


def place_ends(array, rng, low, top_value):
    index_at = [jax.random.randint(jax.random.fold_in(rng, axis), (), 0, length) for axis, length in enumerate(array.shape)]
    main_axis = array.shape.index(max(array.shape))
    beside = index_at[:main_axis] + [(index_at[main_axis] + 1) % array.shape[main_axis]] + index_at[main_axis + 1:]
    return array.at[tuple(index_at)].set(low).at[tuple(beside)].set(top_value)


def with_spikes(result, stream_key, source, target, blocks, factor):
    def block_of(dim):
        return (jnp.arange(result.shape[dim]) // (result.shape[dim] // blocks)).reshape((-1,) + (1,) * (result.ndim - 1 - dim))

    near = jax.random.permutation(stream_key, blocks)[block_of(target)]
    second = (block_of(target) + blocks // 2) % blocks
    return jnp.where((block_of(source) == near) | (block_of(source) == second), factor * result, result)


def level_of(stream_key, extent, cuts, least, largest):
    def one(axis_at, shards_of):
        steps = jax.random.uniform(jax.random.fold_in(jax.random.fold_in(stream_key, 6), axis_at), (shards_of,), jnp.float32, least / len(cuts), largest / len(cuts))
        return jnp.repeat(jnp.exp(steps), extent[axis_at] // shards_of).reshape((-1,) + (1,) * (len(extent) - axis_at - 1))

    level = one(*cuts[0])
    for cut in cuts[1:]:
        level = level * one(*cut)
    return level


def heavy_noise(rng, extent, scale, most, shards, heavy, kind=jnp.bfloat16):
    drawn = scale * jax.random.normal(rng, extent, jnp.float32)
    if shards:
        drawn = drawn * level_of(rng, extent, shards, -0.22, 0.18)
    return jnp.clip(with_spikes(drawn, jax.random.fold_in(rng, 3), *heavy), -most, most).astype(kind)


def setup_inputs(seed: int = 0) -> dict:
    key_list = jax.random.split(jax.random.key(seed), 7)
    grad_parts = heavy_noise(key_list[0], (N_REP, NB, BLK, BLK), (BLK * N_REP) ** -0.5, 0.09375, ((0, 48), (2, 16)), (0, 1, 48, 3.25))
    owner = place_ends(jax.random.randint(key_list[1], (NB,), 0, N_FSDP), jax.random.fold_in(key_list[1], 1), 0, N_FSDP - 1).astype(jnp.int32)
    left_stat = draw_left_stat(jax.random.fold_in(key_list[6], 71), 0)
    right_stat = draw_right_stat(jax.random.fold_in(key_list[6], 71), 0)
    left_root = draw_left_root(jax.random.fold_in(key_list[6], 71), 0)
    right_root = draw_right_root(jax.random.fold_in(key_list[6], 71), 0)
    return dict(grad_parts=grad_parts, owner=owner, left_stat=left_stat, right_stat=right_stat, left_root=left_root, right_root=right_root)


epsilon = 1e-06

def gram_pair(gradient, left_slot, right_slot):
    rows_gram = lax.dot_general(gradient, gradient, (((1,), (1,)), ((), ())), preferred_element_type=jnp.float32)
    cols_gram = lax.dot_general(gradient, gradient, (((0,), (0,)), ((), ())), preferred_element_type=jnp.float32)
    left_out = (left_slot.astype(jnp.float32) + rows_gram).astype(jnp.bfloat16)
    right_out = (right_slot.astype(jnp.float32) + cols_gram).astype(jnp.bfloat16)
    return (left_out, right_out)

def precondition(left_rows, gradient, right_factor):
    middle = jnp.dot(left_rows, gradient, preferred_element_type=jnp.float32).astype(jnp.bfloat16)
    return jnp.dot(middle, right_factor, preferred_element_type=jnp.float32)

def reference(grad_parts, owner, left_stat, right_stat, left_root, right_root):

    def accumulate(carry, partial_value):
        return (carry + partial_value.astype(jnp.float32), None)
    start = jnp.zeros(grad_parts.shape[1:], jnp.float32)
    summed, unused = lax.scan(accumulate, start, grad_parts)
    gradient = summed.astype(jnp.bfloat16)

    def one_group(items):
        block_grad, holder, lefts, rights, left_roots, right_roots = items
        left_slot = lax.dynamic_index_in_dim(lefts, holder, 0, keepdims=False)
        right_slot = lax.dynamic_index_in_dim(rights, holder, 0, keepdims=False)
        left_factor = lax.dynamic_index_in_dim(left_roots, holder, 0, keepdims=False)
        right_factor = lax.dynamic_index_in_dim(right_roots, holder, 0, keepdims=False)
        left_out, right_out = gram_pair(block_grad, left_slot, right_slot)
        product = precondition(left_factor, block_grad, right_factor)
        factor_norm = lax.rsqrt(jnp.mean(product * product) + epsilon)
        return (left_out, right_out, (product * factor_norm).astype(jnp.bfloat16))
    left_upd, right_upd, update = lax.map(one_group, (gradient, owner, left_stat, right_stat, left_root, right_root))
    chosen = jnp.arange(N_FSDP, dtype=jnp.int32)[None, :, None, None] == owner[:, None, None, None]
    left_new = jnp.where(chosen, left_upd[:, None], left_stat)
    right_new = jnp.where(chosen, right_upd[:, None], right_stat)
    return (left_new, right_new, update)
```

```python
import jax
import jax.numpy as jnp
from jax import lax
from jax.sharding import Mesh, PartitionSpec as P

epsilon = 1e-06
AXES = ("zh", "zl", "x", "y", "core")
SIZES = (6, 2, 4, 8, 2)
REP = ("zh", "zl", "x")
FSDP = ("y", "core")


def rotate(value, axis, size, step):
    return lax.ppermute(value, axis, [(i, (i + step) % size) for i in range(size)])


def after(values, event):
    return lax.optimization_barrier((values, event))[0]


def pack(left, right):
    row = lax.broadcasted_iota(jnp.int32, left.shape, 0)
    col = lax.broadcasted_iota(jnp.int32, left.shape, 1)
    both = jnp.where(row <= col, left, right)
    diagonal = jnp.sum(jnp.where(row == col, right, 0).astype(jnp.float32), axis=0)
    diagonal = jnp.broadcast_to(diagonal.astype(jnp.bfloat16)[None], (8, 512))
    upper = jnp.concatenate([both[:256], diagonal], axis=0)
    lower = jnp.concatenate([both[256:], diagonal], axis=0)
    return upper, lower


def unpack(upper, lower):
    both = jnp.concatenate([upper[:256], lower[:256]], axis=0)
    flipped = both.T
    row = lax.broadcasted_iota(jnp.int32, both.shape, 0)
    col = lax.broadcasted_iota(jnp.int32, both.shape, 1)
    left = jnp.where(row <= col, both, flipped)
    right = jnp.where(row == col, upper[256][None], jnp.where(row > col, both, flipped))
    return left, right


def on_device(grad_parts, owner, left_stat, right_stat, left_root, right_root):
    holder = owner[0]
    my_index = lax.axis_index(FSDP)
    y = lax.axis_index("y")
    first = lax.axis_index("core") == 0
    away = lax.rem(y - holder // 2 + 8, 8)
    upper, lower = pack(left_root[0, 0], right_root[0, 0])
    keep = jnp.where(first, upper, lower)
    got = rotate(jnp.where(first, lower, upper), "core", 2, 1)
    here = jnp.where(holder == my_index, keep, got)
    up = rotate(here, "y", 8, 3)
    down = rotate(here, "y", 8, -3)

    parts = grad_parts[0].reshape(6, 8, 32, 512)
    parts = lax.all_to_all(parts, ("zl", "x"), 1, 1, tiled=True)
    parts = jnp.sum(parts.astype(jnp.float32), axis=1).astype(jnp.bfloat16)
    up, down = after((up, down), parts)
    here = jnp.where(away == 0, here, jnp.where(away == 3, up, down))
    up = rotate(here, "y", 8, 1)
    down = rotate(here, "y", 8, -1)
    parts = lax.all_to_all(parts, "zh", 0, 0, tiled=True)
    rows = jnp.sum(parts.astype(jnp.float32), axis=0).astype(jnp.bfloat16)
    gradient = lax.all_gather(rows, FSDP, axis=0, tiled=True)
    up, down = after((up, down), parts)
    here = jnp.where((away == 0) | (away == 3) | (away == 5), here, jnp.where((away == 1) | (away == 4) | (away == 6), up, down))
    other = rotate(here, "core", 2, 1)
    left, right = unpack(jnp.where(first, here, other), jnp.where(first, other, here))

    middle = jnp.dot(left, gradient, preferred_element_type=jnp.float32).astype(jnp.bfloat16)
    product = jnp.dot(middle, right, preferred_element_type=jnp.float32)
    scale = lax.rsqrt(jnp.mean(product * product) + epsilon)
    update = lax.dynamic_slice_in_dim(product, my_index * 32, 32, 0)
    update = (update * scale).astype(jnp.bfloat16)

    owned = holder == my_index
    rows_gram = lax.dot_general(
        gradient, gradient, (((1,), (1,)), ((), ())), preferred_element_type=jnp.float32
    )
    cols_gram = lax.dot_general(
        gradient, gradient, (((0,), (0,)), ((), ())), preferred_element_type=jnp.float32
    )
    left_slot = left_stat[0, 0]
    right_slot = right_stat[0, 0]
    left_out = (left_slot.astype(jnp.float32) + jnp.where(owned, rows_gram, 0.0)).astype(jnp.bfloat16)
    right_out = (right_slot.astype(jnp.float32) + jnp.where(owned, cols_gram, 0.0)).astype(jnp.bfloat16)
    return (left_out[None, None], right_out[None, None], update[None])


def solution(mesh):
    grid = Mesh(mesh.devices.reshape(SIZES), AXES)
    slots = P(REP, FSDP, None, None)
    return jax.shard_map(
        on_device,
        mesh=grid,
        in_specs=(P(REP, None, FSDP, None), P(REP), slots, slots, slots, slots),
        out_specs=(slots, slots, P(REP, FSDP, None)),
        check_vma=False,
    )
```

```python
import jax
import jax.numpy as jnp
from jax import lax
from jax.experimental import pallas as pl
from jax.experimental.pallas import tpu as pltpu
from jax.sharding import Mesh, PartitionSpec as P

epsilon = 1e-06
AXES = ("zh", "zl", "x", "y", "core")
SIZES = (6, 2, 4, 8, 2)
REP = ("zh", "zl", "x")
FSDP = ("y", "core")


def rotate(value, axis, size, step):
    return lax.ppermute(value, axis, [(i, (i + step) % size) for i in range(size)])


def after(values, event):
    return lax.optimization_barrier((values, event))[0]


def pack(left, right):
    row = lax.broadcasted_iota(jnp.int32, left.shape, 0)
    col = lax.broadcasted_iota(jnp.int32, left.shape, 1)
    both = jnp.where(row <= col, left, right)
    diagonal = jnp.sum(jnp.where(row == col, right, 0).astype(jnp.float32), axis=0)
    diagonal = jnp.broadcast_to(diagonal.astype(jnp.bfloat16)[None], (16, 512))
    upper = jnp.concatenate([both[:256], diagonal], axis=0)
    lower = jnp.concatenate([both[256:], diagonal], axis=0)
    return upper, lower


def regroup_kernel(source, target, held, sems):
    into = [
        pltpu.make_async_copy(source.at[:, to], held.at[to], sems.at[0, to]) for to in range(8)
    ]
    out = [pltpu.make_async_copy(held.at[to], target.at[to], sems.at[1, to]) for to in range(8)]
    for copy in into:
        copy.start()
    for to in range(8):
        into[to].wait()
        out[to].start()
    for copy in out:
        copy.wait()


def regroup(parts):
    anywhere = pl.BlockSpec(memory_space=pl.ANY)
    return pl.pallas_call(
        regroup_kernel,
        out_shape=jax.ShapeDtypeStruct((8, 6, 32, 512), jnp.bfloat16),
        in_specs=[anywhere],
        out_specs=anywhere,
        scratch_shapes=[
            pltpu.VMEM((8, 6, 32, 512), jnp.bfloat16),
            pltpu.SemaphoreType.DMA((2, 8)),
        ],
        compiler_params=pltpu.CompilerParams(vmem_limit_bytes=62 * 1024 * 1024),
    )(parts)


def finish_kernel(place, half, other, left_stat, right_stat, left_new, right_new, update,
                  gradient, roots, left_slot, right_slot, product, sems):
    into = [
        pltpu.make_async_copy(left_stat, left_slot, sems.at[0]),
        pltpu.make_async_copy(right_stat, right_slot, sems.at[1]),
    ]
    out = [
        pltpu.make_async_copy(left_slot, left_new, sems.at[2]),
        pltpu.make_async_copy(right_slot, right_new, sems.at[3]),
    ]
    for copy in into:
        copy.start()
    for source, core in ((half, place[2]), (other, 1 - place[2])):
        for y in range(8):
            at = pl.multiple_of((2 * y + core) * 32, 32)
            gradient[pl.ds(at, 32), :] = source[y * 32 : y * 32 + 32, :]
        roots[pl.ds(pl.multiple_of(core * 256, 256), 256), :] = source[256:512, :]
    value = gradient[...]
    owned = place[0] == 1
    for slot, side, arrive, leave in ((left_slot, 1, into[0], out[0]), (right_slot, 0, into[1], out[1])):
        gram = lax.dot_general(
            value, value, (((side,), (side,)), ((), ())), preferred_element_type=jnp.float32
        )
        arrive.wait()

        @pl.when(owned)
        def add():
            slot[...] = (slot[...].astype(jnp.float32) + gram).astype(jnp.bfloat16)

        leave.start()
    both = roots[...]
    diagonal = half[512:528, :].astype(jnp.float32)[0:1, :]
    flipped = both.T.astype(jnp.float32)
    both = both.astype(jnp.float32)
    row = lax.broadcasted_iota(jnp.int32, both.shape, 0)
    col = lax.broadcasted_iota(jnp.int32, both.shape, 1)
    left = jnp.where(row <= col, both, flipped).astype(jnp.bfloat16)
    right = jnp.where(row > col, both, jnp.where(row < col, flipped, diagonal)).astype(jnp.bfloat16)
    middle = jnp.dot(left, value, preferred_element_type=jnp.float32).astype(jnp.bfloat16)
    product[...] = jnp.dot(middle, right, preferred_element_type=jnp.float32)
    total = product[...]
    scale = lax.rsqrt(jnp.sum(total * total, keepdims=True) / (512.0 * 512.0) + epsilon)
    at = pl.multiple_of(place[1] * 32, 32)
    update[...] = (product[pl.ds(at, 32), :] * scale).astype(jnp.bfloat16)
    for copy in out:
        copy.wait()


def finish(place, half, other, left_stat, right_stat):
    square = jax.ShapeDtypeStruct((512, 512), jnp.bfloat16)
    anywhere = pl.BlockSpec(memory_space=pl.ANY)
    vmem = pl.BlockSpec(memory_space=pltpu.VMEM)
    return pl.pallas_call(
        finish_kernel,
        out_shape=(square, square, jax.ShapeDtypeStruct((32, 512), jnp.bfloat16)),
        in_specs=[pl.BlockSpec(memory_space=pltpu.SMEM), vmem, vmem, anywhere, anywhere],
        out_specs=(anywhere, anywhere, vmem),
        scratch_shapes=[
            pltpu.VMEM((512, 512), jnp.bfloat16),
            pltpu.VMEM((512, 512), jnp.bfloat16),
            pltpu.VMEM((512, 512), jnp.bfloat16),
            pltpu.VMEM((512, 512), jnp.bfloat16),
            pltpu.VMEM((512, 512), jnp.float32),
            pltpu.SemaphoreType.DMA((4,)),
        ],
        compiler_params=pltpu.CompilerParams(vmem_limit_bytes=24 * 1024 * 1024),
        cost_estimate=pl.CostEstimate(flops=8 * 512**3, bytes_accessed=4 * 512 * 1024, transcendentals=0),
    )(place, half, other, left_stat, right_stat)


def on_device(grad_parts, owner, left_stat, right_stat, left_root, right_root):
    holder = owner[0]
    my_index = lax.axis_index(FSDP)
    y = lax.axis_index("y")
    first = lax.axis_index("core") == 0
    away = lax.rem(y - holder // 2 + 8, 8)
    place = jnp.stack([(holder == my_index).astype(jnp.int32), my_index, lax.axis_index("core")])

    upper, lower = pack(left_root[0, 0], right_root[0, 0])
    keep = jnp.where(first, upper, lower)
    got = rotate(jnp.where(first, lower, upper), "core", 2, 1)
    here = jnp.where(holder == my_index, keep, got)
    up = rotate(here, "y", 8, 3)
    down = rotate(here, "y", 8, -3)

    parts = regroup(grad_parts[0].reshape(6, 8, 32, 512))
    parts = lax.all_to_all(parts, ("zl", "x"), 0, 0, tiled=True)
    parts = jnp.sum(parts.astype(jnp.float32), axis=0).astype(jnp.bfloat16)
    up, down = after((up, down), parts)
    here = jnp.where(away == 0, here, jnp.where(away == 3, up, down))
    up = rotate(here, "y", 8, 1)
    down = rotate(here, "y", 8, -1)
    parts = lax.all_to_all(parts, "zh", 0, 0, tiled=True)
    rows = jnp.sum(parts.astype(jnp.float32), axis=0).astype(jnp.bfloat16)

    spread = lax.all_to_all(jnp.broadcast_to(rows[None], (8, 32, 512)), "y", 0, 0, tiled=True)
    kept = (away == 0) | (away == 3) | (away == 5)
    here = jnp.where(kept, here, jnp.where((away == 1) | (away == 4) | (away == 6), up, down))
    half = jnp.concatenate([spread.reshape(256, 512), here], axis=0)
    other = rotate(half, "core", 2, 1)
    left_out, right_out, update = finish(place, half, other, left_stat[0, 0], right_stat[0, 0])
    return (left_out[None, None], right_out[None, None], update[None])


def solution(mesh):
    grid = Mesh(mesh.devices.reshape(SIZES), AXES)
    slots = P(REP, FSDP, None, None)
    return jax.shard_map(
        on_device,
        mesh=grid,
        in_specs=(P(REP, None, FSDP, None), P(REP), slots, slots, slots, slots),
        out_specs=(slots, slots, P(REP, FSDP, None)),
        check_vma=False,
    )
```

```python
import jax
import jax.numpy as jnp
from jax import lax
from jax.experimental import pallas as pl
from jax.experimental.pallas import tpu as pltpu
from jax.sharding import Mesh, PartitionSpec as P

epsilon = 1e-06
AXES = ("zh", "zl", "x", "y", "core")
SIZES = (6, 2, 4, 8, 2)
REP = ("zh", "zl", "x")
FSDP = ("y", "core")


def rotate(value, axis, size, step):
    return lax.ppermute(value, axis, [(i, (i + step) % size) for i in range(size)])


def after(values, event):
    return lax.optimization_barrier((values, event))[0]


def pack(left, right):
    row = lax.broadcasted_iota(jnp.int32, left.shape, 0)
    col = lax.broadcasted_iota(jnp.int32, left.shape, 1)
    both = jnp.where(row <= col, left, right)
    diagonal = jnp.sum(jnp.where(row == col, right, 0).astype(jnp.float32), axis=0)
    diagonal = jnp.broadcast_to(diagonal.astype(jnp.bfloat16)[None], (16, 512))
    upper = jnp.concatenate([both[:256], diagonal], axis=0)
    lower = jnp.concatenate([both[256:], diagonal], axis=0)
    return upper, lower


def regroup_kernel(source, target, held, sems):
    into = [
        pltpu.make_async_copy(source.at[:, to], held.at[to], sems.at[0, to]) for to in range(8)
    ]
    out = [pltpu.make_async_copy(held.at[to], target.at[to], sems.at[1, to]) for to in range(8)]
    for copy in into:
        copy.start()
    for to in range(8):
        into[to].wait()
        out[to].start()
    for copy in out:
        copy.wait()


def regroup(parts):
    anywhere = pl.BlockSpec(memory_space=pl.ANY)
    return pl.pallas_call(
        regroup_kernel,
        out_shape=jax.ShapeDtypeStruct((8, 6, 32, 512), jnp.bfloat16),
        in_specs=[anywhere],
        out_specs=anywhere,
        scratch_shapes=[
            pltpu.VMEM((8, 6, 32, 512), jnp.bfloat16),
            pltpu.SemaphoreType.DMA((2, 8)),
        ],
        compiler_params=pltpu.CompilerParams(vmem_limit_bytes=62 * 1024 * 1024),
    )(parts)


def finish_kernel(place, half, other, left_stat, right_stat, left_new, right_new, update,
                  gradient, roots, left_slot, right_slot, product, sems):
    into = [
        pltpu.make_async_copy(left_stat, left_slot, sems.at[0]),
        pltpu.make_async_copy(right_stat, right_slot, sems.at[1]),
    ]
    out = [
        pltpu.make_async_copy(left_slot, left_new, sems.at[2]),
        pltpu.make_async_copy(right_slot, right_new, sems.at[3]),
    ]
    for copy in into:
        copy.start()
    for source, core in ((half, place[2]), (other, 1 - place[2])):
        for y in range(8):
            at = pl.multiple_of((2 * y + core) * 32, 32)
            gradient[pl.ds(at, 32), :] = source[y * 32 : y * 32 + 32, :]
        roots[pl.ds(pl.multiple_of(core * 256, 256), 256), :] = source[256:512, :]
    value = gradient[...]
    both = roots[...]
    diagonal = half[512:528, :].astype(jnp.float32)[0:1, :]
    flipped = both.T.astype(jnp.float32)
    both = both.astype(jnp.float32)
    row = lax.broadcasted_iota(jnp.int32, both.shape, 0)
    col = lax.broadcasted_iota(jnp.int32, both.shape, 1)
    left = jnp.where(row <= col, both, flipped).astype(jnp.bfloat16)
    right = jnp.where(row > col, both, jnp.where(row < col, flipped, diagonal)).astype(jnp.bfloat16)
    middle = jnp.dot(left, value, preferred_element_type=jnp.float32).astype(jnp.bfloat16)
    for slot, side, arrive, leave in ((left_slot, 1, into[0], out[0]), (right_slot, 0, into[1], out[1])):
        arrive.wait()

        @pl.when(place[0] == 1)
        def add():
            gram = lax.dot_general(
                gradient[...], gradient[...], (((side,), (side,)), ((), ())),
                preferred_element_type=jnp.float32,
            )
            slot[...] = (slot[...].astype(jnp.float32) + gram).astype(jnp.bfloat16)

        leave.start()
    product[...] = jnp.dot(middle, right, preferred_element_type=jnp.float32)
    total = product[...]
    scale = lax.rsqrt(jnp.sum(total * total, keepdims=True) / (512.0 * 512.0) + epsilon)
    at = pl.multiple_of(place[1] * 32, 32)
    update[...] = (product[pl.ds(at, 32), :] * scale).astype(jnp.bfloat16)
    for copy in out:
        copy.wait()


def finish(place, half, other, left_stat, right_stat):
    square = jax.ShapeDtypeStruct((512, 512), jnp.bfloat16)
    anywhere = pl.BlockSpec(memory_space=pl.ANY)
    vmem = pl.BlockSpec(memory_space=pltpu.VMEM)
    return pl.pallas_call(
        finish_kernel,
        out_shape=(square, square, jax.ShapeDtypeStruct((32, 512), jnp.bfloat16)),
        in_specs=[pl.BlockSpec(memory_space=pltpu.SMEM), vmem, vmem, anywhere, anywhere],
        out_specs=(anywhere, anywhere, vmem),
        scratch_shapes=[
            pltpu.VMEM((512, 512), jnp.bfloat16),
            pltpu.VMEM((512, 512), jnp.bfloat16),
            pltpu.VMEM((512, 512), jnp.bfloat16),
            pltpu.VMEM((512, 512), jnp.bfloat16),
            pltpu.VMEM((512, 512), jnp.float32),
            pltpu.SemaphoreType.DMA((4,)),
        ],
        compiler_params=pltpu.CompilerParams(vmem_limit_bytes=24 * 1024 * 1024),
        cost_estimate=pl.CostEstimate(flops=8 * 512**3, bytes_accessed=4 * 512 * 1024, transcendentals=0),
    )(place, half, other, left_stat, right_stat)


def on_device(grad_parts, owner, left_stat, right_stat, left_root, right_root):
    holder = owner[0]
    my_index = lax.axis_index(FSDP)
    y = lax.axis_index("y")
    first = lax.axis_index("core") == 0
    away = lax.rem(y - holder // 2 + 8, 8)
    place = jnp.stack([(holder == my_index).astype(jnp.int32), my_index, lax.axis_index("core")])

    upper, lower = pack(left_root[0, 0], right_root[0, 0])
    keep = jnp.where(first, upper, lower)
    got = rotate(jnp.where(first, lower, upper), "core", 2, 1)
    here = jnp.where(holder == my_index, keep, got)
    up = rotate(here, "y", 8, 3)
    down = rotate(here, "y", 8, -2)

    parts = regroup(grad_parts[0].reshape(6, 8, 32, 512))
    parts = lax.all_to_all(parts, ("zl", "x"), 0, 0, tiled=True)
    parts = jnp.sum(parts.astype(jnp.float32), axis=0).astype(jnp.bfloat16)
    up, down = after((up, down), parts)
    here = jnp.where(away == 0, here, jnp.where(away == 3, up, down))
    up = rotate(here, "y", 8, 1)
    down = rotate(here, "y", 8, -1)
    parts = lax.all_to_all(parts, "zh", 0, 0, tiled=True)
    rows = jnp.sum(parts.astype(jnp.float32), axis=0).astype(jnp.bfloat16)

    up, down = after((up, down), parts)
    kept = (away == 0) | (away == 3) | (away == 6)
    here = jnp.where(kept, here, jnp.where((away == 2) | (away == 5), down, up))
    rows, here = lax.optimization_barrier((rows, here))
    spread = lax.all_to_all(jnp.broadcast_to(rows[None], (8, 32, 512)), "y", 0, 0, tiled=True)
    half = jnp.concatenate([spread.reshape(256, 512), here], axis=0)
    other = rotate(half, "core", 2, 1)
    left_out, right_out, update = finish(place, half, other, left_stat[0, 0], right_stat[0, 0])
    return (left_out[None, None], right_out[None, None], update[None])


def solution(mesh):
    grid = Mesh(mesh.devices.reshape(SIZES), AXES)
    slots = P(REP, FSDP, None, None)
    return jax.shard_map(
        on_device,
        mesh=grid,
        in_specs=(P(REP, None, FSDP, None), P(REP), slots, slots, slots, slots),
        out_specs=(slots, slots, P(REP, FSDP, None)),
        check_vma=False,
    )
```

```python
import jax
import jax.numpy as jnp
from jax import lax
from jax.experimental import pallas as pl
from jax.experimental.pallas import tpu as pltpu
from jax.sharding import Mesh, PartitionSpec as P

epsilon = 1e-06
AXES = ("zh", "zl", "x", "y", "core")
SIZES = (6, 2, 4, 8, 2)
REP = ("zh", "zl", "x")
FSDP = ("y", "core")


def rotate(value, axis, size, step):
    return lax.ppermute(value, axis, [(i, (i + step) % size) for i in range(size)])


def after(values, event):
    return lax.optimization_barrier((values, event))[0]


def pack(left, right):
    row = lax.broadcasted_iota(jnp.int32, left.shape, 0)
    col = lax.broadcasted_iota(jnp.int32, left.shape, 1)
    both = jnp.where(row <= col, left, right)
    diagonal = jnp.sum(jnp.where(row == col, right, 0).astype(jnp.float32), axis=0)
    diagonal = jnp.broadcast_to(diagonal.astype(jnp.bfloat16)[None], (16, 512))
    upper = jnp.concatenate([both[:256], diagonal], axis=0)
    lower = jnp.concatenate([both[256:], diagonal], axis=0)
    return upper, lower


def regroup_kernel(source, target, held, sems):
    into, out = [], []
    for to in range(8):
        for part in range(2):
            some = slice(3 * part, 3 * part + 3)
            at = 2 * to + part
            into.append(
                pltpu.make_async_copy(source.at[some, to], held.at[to, some], sems.at[0, at])
            )
            out.append(
                pltpu.make_async_copy(held.at[to, some], target.at[to, some], sems.at[1, at])
            )
    for copy in into:
        copy.start()
    for arrive, leave in zip(into, out):
        arrive.wait()
        leave.start()
    for copy in out:
        copy.wait()


def regroup(parts):
    anywhere = pl.BlockSpec(memory_space=pl.ANY)
    return pl.pallas_call(
        regroup_kernel,
        out_shape=jax.ShapeDtypeStruct((8, 6, 32, 512), jnp.bfloat16),
        in_specs=[anywhere],
        out_specs=anywhere,
        scratch_shapes=[
            pltpu.VMEM((8, 6, 32, 512), jnp.bfloat16),
            pltpu.SemaphoreType.DMA((2, 16)),
        ],
        compiler_params=pltpu.CompilerParams(vmem_limit_bytes=62 * 1024 * 1024),
    )(parts)


def finish_kernel(place, half, other, left_stat, right_stat, left_new, right_new, update,
                  gradient, roots, left_slot, right_slot, product, sems):
    into = [
        pltpu.make_async_copy(left_stat, left_slot, sems.at[0]),
        pltpu.make_async_copy(right_stat, right_slot, sems.at[1]),
    ]
    out = [
        pltpu.make_async_copy(left_slot, left_new, sems.at[2]),
        pltpu.make_async_copy(right_slot, right_new, sems.at[3]),
    ]
    for copy in into:
        copy.start()
    for source, core in ((half, place[2]), (other, 1 - place[2])):
        for y in range(8):
            at = pl.multiple_of((2 * y + core) * 32, 32)
            gradient[pl.ds(at, 32), :] = source[y * 32 : y * 32 + 32, :]
        roots[pl.ds(pl.multiple_of(core * 256, 256), 256), :] = source[256:512, :]
    value = gradient[...]
    both = roots[...]
    diagonal = half[512:528, :].astype(jnp.float32)[0:1, :]
    flipped = both.T.astype(jnp.float32)
    both = both.astype(jnp.float32)
    row = lax.broadcasted_iota(jnp.int32, both.shape, 0)
    col = lax.broadcasted_iota(jnp.int32, both.shape, 1)
    left = jnp.where(row <= col, both, flipped).astype(jnp.bfloat16)
    right = jnp.where(row > col, both, jnp.where(row < col, flipped, diagonal)).astype(jnp.bfloat16)
    middle = jnp.dot(left, value, preferred_element_type=jnp.float32).astype(jnp.bfloat16)
    for slot, side, arrive, leave in ((left_slot, 1, into[0], out[0]), (right_slot, 0, into[1], out[1])):
        arrive.wait()

        @pl.when(place[0] == 1)
        def add():
            gram = lax.dot_general(
                gradient[...], gradient[...], (((side,), (side,)), ((), ())),
                preferred_element_type=jnp.float32,
            )
            slot[...] = (slot[...].astype(jnp.float32) + gram).astype(jnp.bfloat16)

        leave.start()
    product[...] = jnp.dot(middle, right, preferred_element_type=jnp.float32)
    total = product[...]
    scale = lax.rsqrt(jnp.sum(total * total, keepdims=True) / (512.0 * 512.0) + epsilon)
    at = pl.multiple_of(place[1] * 32, 32)
    update[...] = (product[pl.ds(at, 32), :] * scale).astype(jnp.bfloat16)
    for copy in out:
        copy.wait()


def finish(place, half, other, left_stat, right_stat):
    square = jax.ShapeDtypeStruct((512, 512), jnp.bfloat16)
    anywhere = pl.BlockSpec(memory_space=pl.ANY)
    vmem = pl.BlockSpec(memory_space=pltpu.VMEM)
    return pl.pallas_call(
        finish_kernel,
        out_shape=(square, square, jax.ShapeDtypeStruct((32, 512), jnp.bfloat16)),
        in_specs=[pl.BlockSpec(memory_space=pltpu.SMEM), vmem, vmem, anywhere, anywhere],
        out_specs=(anywhere, anywhere, vmem),
        scratch_shapes=[
            pltpu.VMEM((512, 512), jnp.bfloat16),
            pltpu.VMEM((512, 512), jnp.bfloat16),
            pltpu.VMEM((512, 512), jnp.bfloat16),
            pltpu.VMEM((512, 512), jnp.bfloat16),
            pltpu.VMEM((512, 512), jnp.float32),
            pltpu.SemaphoreType.DMA((4,)),
        ],
        compiler_params=pltpu.CompilerParams(vmem_limit_bytes=24 * 1024 * 1024),
        cost_estimate=pl.CostEstimate(flops=8 * 512**3, bytes_accessed=4 * 512 * 1024, transcendentals=0),
    )(place, half, other, left_stat, right_stat)


def on_device(grad_parts, owner, left_stat, right_stat, left_root, right_root):
    holder = owner[0]
    my_index = lax.axis_index(FSDP)
    y = lax.axis_index("y")
    first = lax.axis_index("core") == 0
    away = lax.rem(y - holder // 2 + 8, 8)
    place = jnp.stack([(holder == my_index).astype(jnp.int32), my_index, lax.axis_index("core")])

    upper, lower = pack(left_root[0, 0], right_root[0, 0])
    keep = jnp.where(first, upper, lower)
    got = rotate(jnp.where(first, lower, upper), "core", 2, 1)
    here = jnp.where(holder == my_index, keep, got)
    up = rotate(here, "y", 8, 3)
    down = rotate(here, "y", 8, -2)

    parts = regroup(grad_parts[0].reshape(6, 8, 32, 512))
    parts = lax.all_to_all(parts, ("zl", "x"), 0, 0, tiled=True)
    parts = jnp.sum(parts.astype(jnp.float32), axis=0).astype(jnp.bfloat16)
    up, down = after((up, down), parts)
    here = jnp.where(away == 0, here, jnp.where(away == 3, up, down))
    up = rotate(here, "y", 8, 1)
    down = rotate(here, "y", 8, -1)
    parts = lax.all_to_all(parts, "zh", 0, 0, tiled=True)
    rows = jnp.sum(parts.astype(jnp.float32), axis=0).astype(jnp.bfloat16)

    up, down = after((up, down), parts)
    kept = (away == 0) | (away == 3) | (away == 6)
    here = jnp.where(kept, here, jnp.where((away == 2) | (away == 5), down, up))
    rows, here = lax.optimization_barrier((rows, here))
    spread = lax.all_to_all(jnp.broadcast_to(rows[None], (8, 32, 512)), "y", 0, 0, tiled=True)
    half = jnp.concatenate([spread.reshape(256, 512), here], axis=0)
    other = rotate(half, "core", 2, 1)
    left_out, right_out, update = finish(place, half, other, left_stat[0, 0], right_stat[0, 0])
    return (left_out[None, None], right_out[None, None], update[None])


def solution(mesh):
    grid = Mesh(mesh.devices.reshape(SIZES), AXES)
    slots = P(REP, FSDP, None, None)
    return jax.shard_map(
        on_device,
        mesh=grid,
        in_specs=(P(REP, None, FSDP, None), P(REP), slots, slots, slots, slots),
        out_specs=(slots, slots, P(REP, FSDP, None)),
        check_vma=False,
    )
```
